32 devices in a mesh: row: 2 (over y), col: 8 (over z, core), depth: 2 (over x).
Axes of the slice: x: 2, y: 2, z: 4, core: 2. Of those that a mesh axis runs over, the one named last changes fastest.
Arguments:
- cube: bfloat16 [512, 512, 512], P('row', 'col', 'depth'), may hold values from -18 to 18
- mode3_factor: bfloat16 [512, 256], P('depth'), may hold values from -0.375 to 0.375
- mode2_factor: bfloat16 [512, 256], P('col'), may hold values from -0.375 to 0.375
- start_basis: float32 [512, 256], P('row'), may hold values from -6 to 6
Outputs:
- factor: float32 [512, 256], P('row')
The draws below stay inside these ranges and needn't reach their ends.
All inputs are finite; a program needn't handle non-finite values.
Results may differ from the reference program's by a relative error of at most 0.023.
Values may be sent and summed in bfloat16 or wider, within the bound.
A program may use at most 128 MiB of HBM per device.

```python
import math
import jax
import jax.numpy as jnp
from jax import lax

I1 = 512
RANK = 256
C2 = 64
C3 = 256
ITERS = 4
I2 = 512
I3 = 512
N_COL = 8
N_DEPTH = 2


def draw_cube(key, part):
    key = jax.random.fold_in(key, 11)
    scale_key, value_key = jax.random.split(key)
    spread = jnp.exp(jax.random.uniform(scale_key, (I1, 1, 1), jnp.float32, 0.0, 1.0986123))
    values = jnp.clip(jax.random.normal(value_key, (I1, I2, I3), jnp.float32), -6.0, 6.0)
    return (values * spread).astype(jnp.bfloat16)


def with_spikes(result, stream_key, source, target, parts, factor):
    def block_of(position):
        return (jnp.arange(result.shape[position]) // (result.shape[position] // parts)).reshape((-1,) + (1,) * (result.ndim - 1 - position))

    first = jax.random.permutation(stream_key, parts)[block_of(target)]
    second = (block_of(target) + parts // 2) % parts
    return jnp.where((block_of(source) == first) | (block_of(source) == second), factor * result, result)


def level_of(own_key, dims, shards, smallest, top_value):
    def one(position, parts):
        steps = jax.random.uniform(jax.random.fold_in(jax.random.fold_in(own_key, 6), position), (parts,), jnp.float32, smallest / len(shards), top_value / len(shards))
        return jnp.repeat(jnp.exp(steps), dims[position] // parts).reshape((-1,) + (1,) * (len(dims) - position - 1))

    gain = one(*shards[0])
    for cut in shards[1:]:
        gain = gain * one(*cut)
    return gain


def gaussian(own_key, extent, deviation, bound, cuts=(), held_as=jnp.bfloat16):
    level = level_of(own_key, extent, cuts, -0.22, 0.18) if cuts else 1.0
    drawn = jax.random.normal(own_key, extent, jnp.float32) * deviation * level
    return jnp.minimum(jnp.maximum(drawn, -bound), bound).astype(held_as)


def heavy_noise(stream_key, shape, scale, bound, shards, heavy, held_as=jnp.bfloat16):
    values = scale * jax.random.normal(stream_key, shape, jnp.float32)
    if shards:
        values = values * level_of(stream_key, shape, shards, -0.22, 0.18)
    return jnp.clip(with_spikes(values, jax.random.fold_in(stream_key, 3), *heavy), -bound, bound).astype(held_as)


def setup_inputs(seed: int = 0) -> dict:
    arg_keys = jax.random.split(jax.random.key(seed), 5)
    return {
        "cube": draw_cube(jax.random.fold_in(arg_keys[4], 71), 0),
        "mode3_factor": heavy_noise(arg_keys[1], (I3, RANK), I3 ** -0.5, 0.375, ((0, 2),), (0, 1, 2, 2.0)),
        "mode2_factor": heavy_noise(arg_keys[2], (I2, RANK), I2 ** -0.5, 0.375, ((0, 8),), (0, 1, 8, 2.0)),
        "start_basis": gaussian(arg_keys[3], (I1, RANK), 1.0, 6.0, ((0, 2),), jnp.float32),
    }


def reference(cube, mode3_factor, mode2_factor, start_basis):
    middle_sum = jnp.zeros((I1 * I2, RANK), jnp.float32)
    for block in range(N_DEPTH):
        piece = cube[:, :, block * C3:(block + 1) * C3].reshape(I1 * I2, C3)
        term = jnp.dot(piece.astype(jnp.float32), mode3_factor[block * C3:(block + 1) * C3].astype(jnp.float32), preferred_element_type=jnp.float32)
        middle_sum = middle_sum + term.astype(jnp.bfloat16).astype(jnp.float32)
    middle = middle_sum.astype(jnp.bfloat16).reshape(I1, I2, RANK)
    middle_t = jnp.transpose(middle, (0, 2, 1))
    core_sum = jnp.zeros((I1 * RANK, RANK), jnp.float32)
    for block in range(N_COL):
        piece = middle_t[:, :, block * C2:(block + 1) * C2].reshape(I1 * RANK, C2)
        term = jnp.dot(piece.astype(jnp.float32), mode2_factor[block * C2:(block + 1) * C2].astype(jnp.float32), preferred_element_type=jnp.float32)
        core_sum = core_sum + term.astype(jnp.bfloat16).astype(jnp.float32)
    core = core_sum.astype(jnp.bfloat16).reshape(I1, RANK * RANK)
    gram = jnp.dot(core.astype(jnp.float32), core.T.astype(jnp.float32), preferred_element_type=jnp.float32)
    basis = start_basis
    for step in range(ITERS):
        image = jnp.dot(gram, basis, precision=lax.Precision.HIGHEST)
        cross = jnp.dot(image.T, image, precision=lax.Precision.HIGHEST)
        lower = jnp.linalg.cholesky(cross)
        basis = jax.scipy.linalg.solve_triangular(lower, image.T, lower=True).T
    return basis * math.sqrt(I1)
```

```python
import functools
import math

import jax
import jax.numpy as jnp
from jax import lax
from jax.experimental import pallas as pl
from jax.experimental.pallas import tpu as pltpu
from jax.sharding import PartitionSpec as P

ITERS = 4
OUTER = 64
HIGHEST = lax.Precision.HIGHEST


def dot(a, b, ca, cb, precision=HIGHEST):
    return lax.dot_general(
        a, b, (((ca,), (cb,)), ((), ())), precision=precision, preferred_element_type=jnp.float32
    )


def block_inverse(block):
    n = OUTER
    lane = lax.broadcasted_iota(jnp.int32, (n, n), 1)
    sub = lax.broadcasted_iota(jnp.int32, (n, n), 0)
    eye = jnp.where(lane == sub, 1.0, 0.0).astype(jnp.float32)
    whole = jnp.concatenate([block, eye], axis=1)
    tiles = [whole[8 * v : 8 * v + 8, :] for v in range(n // 8)]
    sublane = lax.broadcasted_iota(jnp.int32, (8, 2 * n), 0)
    full = (8, 2 * n)
    for b in range(n // 8):
        tile = tiles[b]
        d = {}
        for j in range(8):
            column = jnp.broadcast_to(tile[:, 8 * b + j : 8 * b + j + 1], full)
            for i in range(j, 8):
                d[i, j] = jnp.broadcast_to(column[i : i + 1, :], full)
        rows = [jnp.broadcast_to(tile[k : k + 1, :], full) for k in range(8)]
        low, p, reduced = {}, [], []
        for j in range(8):
            p.append(lax.rsqrt(d[j, j]))
            for i in range(j + 1, 8):
                low[i, j] = d[i, j] * p[j]
            for k in range(j + 1, 8):
                for i in range(k, 8):
                    d[i, k] = d[i, k] - low[i, j] * low[k, j]
            row = rows[j] * p[j]
            reduced.append(row)
            for i in range(j + 1, 8):
                rows[i] = rows[i] - low[i, j] * row
        out = reduced[0]
        for k in range(1, 8):
            out = jnp.where(sublane == k, reduced[k], out)
        tiles[b] = out
        if b < n // 8 - 1:
            solved = list(reduced)
            for k in range(7, -1, -1):
                solved[k] = solved[k] * p[k]
                for m in range(k):
                    solved[m] = solved[m] - low[k, m] * solved[k]
            for v in range(b + 1, n // 8):
                old = tiles[v]
                new = old
                for k in range(8):
                    new = new - jnp.broadcast_to(old[:, 8 * b + k : 8 * b + k + 1], full) * solved[k]
                tiles[v] = new
    return jnp.concatenate(tiles, axis=0)[:, n:]


def subspace_kernel(gram_ref, start_ref, out_ref, image_ref, work_ref, block_ref):
    size = start_ref.shape[1]
    out_ref[...] = start_ref[...]
    blocks = size // OUTER

    def iteration(step, carry):
        image_ref[...] = dot(gram_ref[...], out_ref[...], 1, 0)
        image = image_ref[...]
        work_ref[:, :size] = dot(image, image, 0, 0)
        lane = lax.broadcasted_iota(jnp.int32, (size, size), 1)
        sub = lax.broadcasted_iota(jnp.int32, (size, size), 0)
        work_ref[:, size:] = jnp.where(lane == sub, 1.0, 0.0).astype(jnp.float32)
        block_ref[...] = work_ref[:OUTER, :OUTER]

        def outer(o, carry):
            inverse = block_inverse(block_ref[...])
            for s in range(blocks):

                @pl.when(o == s)
                def _():
                    low, high = s * OUTER, (s + 1) * OUTER
                    rows = dot(inverse, work_ref[low:high, :], 1, 0)
                    work_ref[low:high, :] = rows
                    if s < blocks - 1:
                        work_ref[high:, :] -= dot(rows[:, high:size], rows, 0, 0)
                        block_ref[...] = work_ref[high : high + OUTER, high : high + OUTER]

            return carry

        lax.fori_loop(0, blocks, outer, 0)
        scale = jnp.where(step == ITERS - 1, math.sqrt(gram_ref.shape[0]), 1.0).astype(jnp.float32)
        out_ref[...] = dot(image_ref[...], work_ref[:, size:], 1, 1) * scale
        return carry

    lax.fori_loop(0, ITERS, iteration, 0)


def subspace(gram, start):
    length, size = start.shape
    return pl.pallas_call(
        subspace_kernel,
        out_shape=jax.ShapeDtypeStruct((length, size), jnp.float32),
        in_specs=[pl.BlockSpec(memory_space=pltpu.VMEM)] * 2,
        out_specs=pl.BlockSpec(memory_space=pltpu.VMEM),
        scratch_shapes=[
            pltpu.VMEM((length, size), jnp.float32),
            pltpu.VMEM((size, 2 * size), jnp.float32),
            pltpu.VMEM((OUTER, OUTER), jnp.float32),
        ],
        compiler_params=pltpu.CompilerParams(vmem_limit_bytes=40 * 2**20),
        name="subspace",
    )(gram, start)


def shards(cube, mode3_factor, mode2_factor, start_basis):
    rows, width2, width3 = cube.shape
    rank = mode3_factor.shape[1]
    n_depth = lax.axis_size("depth")
    flat = cube.reshape(rows * width2, width3)
    rank3 = rank // n_depth
    middle = lax.psum_scatter(
        lax.dot_general(
            mode3_factor, flat, (((0,), (1,)), ((), ())), preferred_element_type=jnp.float32
        ).astype(jnp.bfloat16),
        "depth",
        scatter_dimension=0,
        tiled=True,
    )
    middle = middle.reshape(rank3, rows, width2)
    middle = lax.all_to_all(middle, "col", 0, 2, tiled=True)
    factor2 = lax.all_gather(mode2_factor, "col", axis=0, tiled=True)
    core = jnp.einsum("tij,jr->tri", middle, factor2, preferred_element_type=jnp.float32)
    core = core.astype(jnp.bfloat16)
    core = lax.all_to_all(core, "row", 1, 2, tiled=True)
    core = core.reshape(-1, core.shape[2])
    gram = lax.psum(dot(core, core, 0, 0, None), ("row", "col", "depth"))
    start = lax.all_gather(start_basis, "row", axis=0, tiled=True)
    basis = subspace(gram, start)
    return lax.dynamic_slice_in_dim(basis, lax.axis_index("row") * rows, rows, 0)


def solution(mesh):
    in_specs = (P("row", "col", "depth"), P("depth", None), P("col", None), P("row", None))
    out_specs = P("row", None)
    return jax.shard_map(shards, mesh=mesh, in_specs=in_specs, out_specs=out_specs, check_vma=False)
```

```python
import functools
import math

import jax
import jax.numpy as jnp
from jax import lax
from jax.experimental import pallas as pl
from jax.experimental.pallas import tpu as pltpu
from jax.sharding import PartitionSpec as P

ITERS = 4
OUTER = 64
HIGHEST = lax.Precision.HIGHEST


def dot(a, b, ca, cb, precision=HIGHEST):
    return lax.dot_general(
        a, b, (((ca,), (cb,)), ((), ())), precision=precision, preferred_element_type=jnp.float32
    )


def block_inverse(block):
    n = OUTER
    lane = lax.broadcasted_iota(jnp.int32, (n, n), 1)
    sub = lax.broadcasted_iota(jnp.int32, (n, n), 0)
    eye = jnp.where(lane == sub, 1.0, 0.0).astype(jnp.float32)
    whole = jnp.concatenate([block, eye], axis=1)
    tiles = [whole[8 * v : 8 * v + 8, :] for v in range(n // 8)]
    sublane = lax.broadcasted_iota(jnp.int32, (8, 2 * n), 0)
    full = (8, 2 * n)
    for b in range(n // 8):
        tile = tiles[b]
        d = {}
        for j in range(8):
            column = jnp.broadcast_to(tile[:, 8 * b + j : 8 * b + j + 1], full)
            for i in range(j, 8):
                d[i, j] = jnp.broadcast_to(column[i : i + 1, :], full)
        rows = [jnp.broadcast_to(tile[k : k + 1, :], full) for k in range(8)]
        low, p, reduced = {}, [], []
        for j in range(8):
            p.append(lax.rsqrt(d[j, j]))
            for i in range(j + 1, 8):
                low[i, j] = d[i, j] * p[j]
            for k in range(j + 1, 8):
                for i in range(k, 8):
                    d[i, k] = d[i, k] - low[i, j] * low[k, j]
            row = rows[j] * p[j]
            reduced.append(row)
            for i in range(j + 1, 8):
                rows[i] = rows[i] - low[i, j] * row
        out = reduced[0]
        for k in range(1, 8):
            out = jnp.where(sublane == k, reduced[k], out)
        tiles[b] = out
        if b < n // 8 - 1:
            solved = list(reduced)
            for k in range(7, -1, -1):
                solved[k] = solved[k] * p[k]
                for m in range(k):
                    solved[m] = solved[m] - low[k, m] * solved[k]
            for v in range(b + 1, n // 8):
                old = tiles[v]
                new = old
                for k in range(8):
                    new = new - jnp.broadcast_to(old[:, 8 * b + k : 8 * b + k + 1], full) * solved[k]
                tiles[v] = new
    return jnp.concatenate(tiles, axis=0)[:, n:]


def subspace_kernel(gram_ref, start_ref, out_ref, image_ref, work_ref, block_ref):
    size = start_ref.shape[1]
    out_ref[...] = start_ref[...]
    blocks = size // OUTER

    def iteration(step, carry):
        image_ref[...] = dot(gram_ref[...], out_ref[...], 1, 0)
        image = image_ref[...]
        work_ref[:, :size] = dot(image, image, 0, 0)
        lane = lax.broadcasted_iota(jnp.int32, (size, size), 1)
        sub = lax.broadcasted_iota(jnp.int32, (size, size), 0)
        work_ref[:, size:] = jnp.where(lane == sub, 1.0, 0.0).astype(jnp.float32)
        block_ref[...] = work_ref[:OUTER, :OUTER]

        def outer(o, carry):
            inverse = block_inverse(block_ref[...])
            for s in range(blocks):

                @pl.when(o == s)
                def _():
                    low, high = s * OUTER, (s + 1) * OUTER
                    rows = dot(inverse, work_ref[low:high, :], 1, 0)
                    work_ref[low:high, :] = rows
                    if s < blocks - 1:
                        work_ref[high:, :] -= dot(rows[:, high:size], rows, 0, 0)
                        block_ref[...] = work_ref[high : high + OUTER, high : high + OUTER]

            return carry

        lax.fori_loop(0, blocks, outer, 0)
        scale = jnp.where(step == ITERS - 1, math.sqrt(gram_ref.shape[0]), 1.0).astype(jnp.float32)
        out_ref[...] = dot(image_ref[...], work_ref[:, size:], 1, 1) * scale
        return carry

    lax.fori_loop(0, ITERS, iteration, 0)


def subspace(gram, start):
    length, size = start.shape
    return pl.pallas_call(
        subspace_kernel,
        out_shape=jax.ShapeDtypeStruct((length, size), jnp.float32),
        in_specs=[pl.BlockSpec(memory_space=pltpu.VMEM)] * 2,
        out_specs=pl.BlockSpec(memory_space=pltpu.VMEM),
        scratch_shapes=[
            pltpu.VMEM((length, size), jnp.float32),
            pltpu.VMEM((size, 2 * size), jnp.float32),
            pltpu.VMEM((OUTER, OUTER), jnp.float32),
        ],
        compiler_params=pltpu.CompilerParams(vmem_limit_bytes=40 * 2**20),
        name="subspace",
    )(gram, start)


CHUNKS = 4
MESH = pl.DeviceIdType.MESH


def exchange_kernel(
    sizes, cube_ref, m3_ref, m2_ref, start_ref, gram_out, start_out,
    flat, outgoing, from_depth, middle, gathered, m2_all, m2_t, core, pairs, gram, start_all,
    from_core, part, from_group, reduced, total,
    x_send, x_recv, z_send, z_recv, y_send, y_recv, m_send, m_recv, s_send, s_recv,
    c_send, c_recv, g_send, g_recv,
):
    n_row, n_col, n_depth = sizes
    width2, rows, width3 = cube_ref.shape
    per = middle.shape[2]
    count = n_depth * n_col * per
    rank2 = m2_ref.shape[1]
    half2 = rank2 // n_row
    row, col, depth = lax.axis_index("row"), lax.axis_index("col"), lax.axis_index("depth")
    n_z = n_col // 2
    z, parity = col // 2, col % 2
    other_row, other_depth = 1 - row, 1 - depth

    barrier = pltpu.get_barrier_semaphore()
    others = 0
    for dr in range(n_row):
        for dc in range(n_col):
            for dd in range(n_depth):
                if dr or dc or dd:
                    target = ((row + dr) % n_row, (col + dc) % n_col, (depth + dd) % n_depth)
                    pl.semaphore_signal(barrier, inc=1, device_id=target, device_id_type=MESH)
                    others += 1
    pl.semaphore_wait(barrier, others)

    started = []

    def send(src, dst, send_sem, recv_sem, target):
        copy = pltpu.make_async_remote_copy(
            src_ref=src, dst_ref=dst, send_sem=send_sem, recv_sem=recv_sem,
            device_id=target, device_id_type=MESH,
        )
        copy.start()
        started.append(copy)
        return copy

    own2 = pl.ds(pl.multiple_of(col * width2, width2), width2)
    m_copies = [
        send(m2_ref, m2_all.at[own2, :], m_send.at[o], m_recv.at[o], (row, (col + o) % n_col, depth))
        for o in range(1, n_col)
    ]
    own_rows = pl.ds(pl.multiple_of(row * rows, rows), rows)
    s_copy = send(start_ref, start_all.at[own_rows, :], s_send, s_recv, (other_row, col, depth))
    m2_all[own2, :] = m2_ref[...]
    start_all[own_rows, :] = start_ref[...]
    gram[...] = jnp.zeros_like(gram)
    x_copies, z_copies, y_copies = {}, {}, {}

    def first(q):
        def multiply(j, carry):
            tile = dot(m3_ref[q], cube_ref[j], 1, 1, None)
            for h in range(rows // 128):
                flat[h, pl.ds(j, count, stride=width2), :] = tile[:, h * 128 : h * 128 + 128]
            return carry

        lax.fori_loop(0, width2, multiply, 0, unroll=4)
        for d in range(n_depth):

            def store(t, carry):
                at = pl.ds(pl.multiple_of((d * n_col * per + t) * width2, width2), width2)
                for h in range(rows // 128):
                    outgoing[q, d, t, :, h * 128 : h * 128 + 128] = flat[h, at, :].astype(jnp.bfloat16)
                return carry

            lax.fori_loop(0, n_col * per, store, 0)
        x_copies[q] = send(
            outgoing.at[q, other_depth], from_depth.at[q], x_send.at[q], x_recv.at[q],
            (row, col, other_depth),
        )

    def second(q):
        x_copies[q].wait_recv()

        for c in range(n_col):
            for t in range(per):
                a = outgoing[q, depth, c * per + t].astype(jnp.float32)
                b = from_depth[q, c * per + t].astype(jnp.float32)
                middle[q, c, t] = (a + b).astype(jnp.bfloat16)
        z_copies[q] = []
        for o in range(1, n_col):
            to = (col + o) % n_col
            z_copies[q].append(
                send(
                    middle.at[q, to], gathered.at[q, :, own2, :], z_send.at[q, o], z_recv.at[q, o],
                    (row, to, depth),
                )
            )
        gathered[q, :, own2, :] = middle[q, col]

    def third(q):
        if q == 0:
            for copy in m_copies:
                copy.wait_recv()
            m2_t[...] = m2_all[...].astype(jnp.float32).T.astype(jnp.bfloat16)
        for copy in z_copies[q]:
            copy.wait_recv()

        def multiply(t, carry):
            core[q, t] = dot(m2_t[...], gathered[q, t], 1, 0, None).astype(jnp.bfloat16)
            return carry

        lax.fori_loop(0, per, multiply, 0)
        mine = pl.ds(pl.multiple_of(row * half2, half2), half2)
        theirs = pl.ds(pl.multiple_of(other_row * half2, half2), half2)
        lanes = pl.ds(pl.multiple_of(row * rows, rows), rows)
        y_copies[q] = send(
            core.at[q, :, theirs, :], pairs.at[q, :, :, lanes], y_send.at[q], y_recv.at[q],
            (other_row, col, depth),
        )
        pairs[q, :, :, lanes] = core[q, :, mine, :]

    def fourth(q):
        y_copies[q].wait_recv()
        x = pairs[q].reshape(per * half2, n_row * rows)
        gram[...] += dot(x, x, 0, 0, None)

    stages = [first, second, third, fourth]
    for wave in range(CHUNKS + 3):
        for stage in range(4):
            if 0 <= wave - stage < CHUNKS:
                stages[stage](wave - stage)

    length = gram.shape[0]
    half = length // 2
    piece = half // (n_row * n_z * n_depth)

    def group(r, zz, d):
        return (r * n_z + zz) * n_depth + d

    keep = pl.ds(pl.multiple_of(parity * half, half), half)
    give = pl.ds(pl.multiple_of((1 - parity) * half, half), half)
    partner = (row, z * 2 + 1 - parity, depth)
    copy = send(gram.at[give, :], from_core, c_send.at[0], c_recv.at[0], partner)
    copy.wait_recv()
    part[...] = gram[keep, :] + from_core[...]
    offsets = [
        (dr, dz, dd)
        for dz in range(n_z) for dr in range(n_row) for dd in range(n_depth) if dr or dz or dd
    ]
    me = group(row, z, depth)
    copies = []
    for k, (dr, dz, dd) in enumerate(offsets):
        r, zz, d = (row + dr) % n_row, (z + dz) % n_z, (depth + dd) % n_depth
        at = pl.ds(pl.multiple_of(group(r, zz, d) * piece, piece), piece)
        copies.append(
            send(part.at[at, :], from_group.at[k], g_send.at[0, k], g_recv.at[0, k], (r, zz * 2 + parity, d))
        )
    value = part[pl.ds(pl.multiple_of(me * piece, piece), piece), :]
    for k, copy in enumerate(copies):
        copy.wait_recv()
        value = value + from_group[k]
    reduced[...] = value
    here = pl.ds(pl.multiple_of(parity * half + me * piece, piece), piece)
    copies = []
    for k, (dr, dz, dd) in enumerate(offsets):
        r, zz, d = (row + dr) % n_row, (z + dz) % n_z, (depth + dd) % n_depth
        copies.append(
            send(reduced, total.at[here, :], g_send.at[1, k], g_recv.at[1, k], (r, zz * 2 + parity, d))
        )
    total[here, :] = value
    for copy in copies:
        copy.wait_recv()
    copy = send(total.at[keep, :], total.at[keep, :], c_send.at[1], c_recv.at[1], partner)
    s_copy.wait_recv()
    start_out[...] = start_all[...]
    copy.wait_recv()
    gram_out[...] = total[...]
    for copy in started:
        copy.wait_send()


def exchange(sizes, cube, mode3_factor, mode2_factor, start_basis):
    n_row, n_col, n_depth = sizes
    rows, width2, width3 = cube.shape
    rank3, rank2 = mode3_factor.shape[1], mode2_factor.shape[1]
    per = rank3 // (n_depth * n_col * CHUNKS)
    cube_t = jnp.swapaxes(cube, 0, 1)
    m3 = mode3_factor.T.reshape(n_depth, n_col, CHUNKS, per, width3)
    m3 = m3.transpose(2, 0, 1, 3, 4).reshape(CHUNKS, n_depth * n_col * per, width3)
    length, half2 = n_row * rows, rank2 // n_row
    count = n_depth * n_col * per
    group = n_row * n_col // 2 * n_depth
    piece = length // 2 // group
    bf16, f32, dma = jnp.bfloat16, jnp.float32, pltpu.SemaphoreType.DMA
    vmem = pl.BlockSpec(memory_space=pltpu.VMEM)
    return pl.pallas_call(
        functools.partial(exchange_kernel, sizes),
        out_shape=[
            jax.ShapeDtypeStruct((length, length), f32),
            jax.ShapeDtypeStruct((length, start_basis.shape[1]), f32),
        ],
        in_specs=[vmem] * 4,
        out_specs=[vmem] * 2,
        scratch_shapes=[
            pltpu.VMEM((rows // 128, count * width2, 128), f32),
            pltpu.VMEM((CHUNKS, n_depth, n_col * per, width2, rows), bf16),
            pltpu.VMEM((CHUNKS, n_col * per, width2, rows), bf16),
            pltpu.VMEM((CHUNKS, n_col, per, width2, rows), bf16),
            pltpu.VMEM((CHUNKS, per, n_col * width2, rows), bf16),
            pltpu.VMEM((n_col * width2, rank2), bf16),
            pltpu.VMEM((rank2, n_col * width2), bf16),
            pltpu.VMEM((CHUNKS, per, rank2, rows), bf16),
            pltpu.VMEM((CHUNKS, per, half2, length), bf16),
            pltpu.VMEM((length, length), f32),
            pltpu.VMEM((length, start_basis.shape[1]), f32),
            pltpu.VMEM((length // 2, length), f32),
            pltpu.VMEM((length // 2, length), f32),
            pltpu.VMEM((group - 1, piece, length), f32),
            pltpu.VMEM((piece, length), f32),
            pltpu.VMEM((length, length), f32),
            dma((CHUNKS,)), dma((CHUNKS,)), dma((CHUNKS, n_col)), dma((CHUNKS, n_col)),
            dma((CHUNKS,)), dma((CHUNKS,)), dma((n_col,)), dma((n_col,)), dma, dma,
            dma((2,)), dma((2,)), dma((2, group)), dma((2, group)),
        ],
        compiler_params=pltpu.CompilerParams(
            collective_id=0, has_side_effects=True, vmem_limit_bytes=60 * 2**20
        ),
        name="exchange",
    )(cube_t, m3, mode2_factor, start_basis)


def collectives(cube, mode3_factor, mode2_factor, start_basis):
    rows, width2, width3 = cube.shape
    rank = mode3_factor.shape[1]
    n_depth = lax.axis_size("depth")
    flat = cube.reshape(rows * width2, width3)
    rank3 = rank // n_depth
    middle = lax.psum_scatter(
        lax.dot_general(
            mode3_factor, flat, (((0,), (1,)), ((), ())), preferred_element_type=jnp.float32
        ).astype(jnp.bfloat16),
        "depth",
        scatter_dimension=0,
        tiled=True,
    )
    middle = middle.reshape(rank3, rows, width2)
    middle = lax.all_to_all(middle, "col", 0, 2, tiled=True)
    factor2 = lax.all_gather(mode2_factor, "col", axis=0, tiled=True)
    core = jnp.einsum("tij,jr->tri", middle, factor2, preferred_element_type=jnp.float32)
    core = core.astype(jnp.bfloat16)
    core = lax.all_to_all(core, "row", 1, 2, tiled=True)
    core = core.reshape(-1, core.shape[2])
    gram = lax.psum(dot(core, core, 0, 0, None), ("row", "col", "depth"))
    start = lax.all_gather(start_basis, "row", axis=0, tiled=True)
    return gram, start


def shards(cube, mode3_factor, mode2_factor, start_basis):
    rows = cube.shape[0]
    sizes = tuple(lax.axis_size(name) for name in ("row", "col", "depth"))
    if sizes[0] == 2 and sizes[2] == 2 and rows % 128 == 0 and rows * 2 % (16 * sizes[1] * 4) == 0:
        gram, start = exchange(sizes, cube, mode3_factor, mode2_factor, start_basis)
    else:
        gram, start = collectives(cube, mode3_factor, mode2_factor, start_basis)
    basis = subspace(gram, start)
    return lax.dynamic_slice_in_dim(basis, lax.axis_index("row") * rows, rows, 0)


def solution(mesh):
    in_specs = (P("row", "col", "depth"), P("depth", None), P("col", None), P("row", None))
    out_specs = P("row", None)
    return jax.shard_map(shards, mesh=mesh, in_specs=in_specs, out_specs=out_specs, check_vma=False)
```

```python
import functools
import math

import jax
import jax.numpy as jnp
from jax import lax
from jax.experimental import pallas as pl
from jax.experimental.pallas import tpu as pltpu
from jax.sharding import PartitionSpec as P

ITERS = 4
OUTER = 128
HIGHEST = lax.Precision.HIGHEST


def dot(a, b, ca, cb, precision=HIGHEST):
    return lax.dot_general(
        a, b, (((ca,), (cb,)), ((), ())), precision=precision, preferred_element_type=jnp.float32
    )


def block_inverse(block):
    n = OUTER
    lane = lax.broadcasted_iota(jnp.int32, (n, n), 1)
    sub = lax.broadcasted_iota(jnp.int32, (n, n), 0)
    eye = jnp.where(lane == sub, 1.0, 0.0).astype(jnp.float32)
    whole = jnp.concatenate([block, eye], axis=1)
    tiles = [whole[8 * v : 8 * v + 8, :] for v in range(n // 8)]
    sublane = lax.broadcasted_iota(jnp.int32, (8, 2 * n), 0)
    full = (8, 2 * n)
    for b in range(n // 8):
        tile = tiles[b]
        d = {}
        for j in range(8):
            column = jnp.broadcast_to(tile[:, 8 * b + j : 8 * b + j + 1], full)
            for i in range(j, 8):
                d[i, j] = jnp.broadcast_to(column[i : i + 1, :], full)
        rows = [jnp.broadcast_to(tile[k : k + 1, :], full) for k in range(8)]
        low, p, reduced = {}, [], []
        for j in range(8):
            p.append(lax.rsqrt(d[j, j]))
            for i in range(j + 1, 8):
                low[i, j] = d[i, j] * p[j]
            for k in range(j + 1, 8):
                for i in range(k, 8):
                    d[i, k] = d[i, k] - low[i, j] * low[k, j]
            row = rows[j] * p[j]
            reduced.append(row)
            for i in range(j + 1, 8):
                rows[i] = rows[i] - low[i, j] * row
        out = reduced[0]
        for k in range(1, 8):
            out = jnp.where(sublane == k, reduced[k], out)
        tiles[b] = out
        if b < n // 8 - 1:
            solved = list(reduced)
            for k in range(7, -1, -1):
                solved[k] = solved[k] * p[k]
                for m in range(k):
                    solved[m] = solved[m] - low[k, m] * solved[k]
            for v in range(b + 1, n // 8):
                old = tiles[v]
                new = old
                for k in range(8):
                    new = new - jnp.broadcast_to(old[:, 8 * b + k : 8 * b + k + 1], full) * solved[k]
                tiles[v] = new
    return jnp.concatenate(tiles, axis=0)[:, n:]


def subspace_kernel(gram_ref, start_ref, out_ref, image_ref, work_ref, block_ref):
    size = start_ref.shape[1]
    out_ref[...] = start_ref[...]
    blocks = size // OUTER

    def iteration(step, carry):
        image_ref[...] = dot(gram_ref[...], out_ref[...], 1, 0)
        image = image_ref[...]
        work_ref[:, :size] = dot(image, image, 0, 0)
        lane = lax.broadcasted_iota(jnp.int32, (size, size), 1)
        sub = lax.broadcasted_iota(jnp.int32, (size, size), 0)
        work_ref[:, size:] = jnp.where(lane == sub, 1.0, 0.0).astype(jnp.float32)
        block_ref[...] = work_ref[:OUTER, :OUTER]

        def outer(o, carry):
            inverse = block_inverse(block_ref[...])
            for s in range(blocks):

                @pl.when(o == s)
                def _():
                    low, high = s * OUTER, (s + 1) * OUTER
                    rows = dot(inverse, work_ref[low:high, :], 1, 0)
                    work_ref[low:high, :] = rows
                    if s < blocks - 1:
                        work_ref[high:, :] -= dot(rows[:, high:size], rows, 0, 0)
                        block_ref[...] = work_ref[high : high + OUTER, high : high + OUTER]

            return carry

        lax.fori_loop(0, blocks, outer, 0)
        scale = jnp.where(step == ITERS - 1, math.sqrt(gram_ref.shape[0]), 1.0).astype(jnp.float32)
        out_ref[...] = dot(image_ref[...], work_ref[:, size:], 1, 1) * scale
        return carry

    lax.fori_loop(0, ITERS, iteration, 0)


def subspace(gram, start):
    length, size = start.shape
    return pl.pallas_call(
        subspace_kernel,
        out_shape=jax.ShapeDtypeStruct((length, size), jnp.float32),
        in_specs=[pl.BlockSpec(memory_space=pltpu.VMEM)] * 2,
        out_specs=pl.BlockSpec(memory_space=pltpu.VMEM),
        scratch_shapes=[
            pltpu.VMEM((length, size), jnp.float32),
            pltpu.VMEM((size, 2 * size), jnp.float32),
            pltpu.VMEM((OUTER, OUTER), jnp.float32),
        ],
        compiler_params=pltpu.CompilerParams(vmem_limit_bytes=40 * 2**20),
        name="subspace",
    )(gram, start)


CHUNKS = 8
MESH = pl.DeviceIdType.MESH


def exchange_kernel(
    sizes, cube_ref, m3_ref, m2_ref, start_ref, gram_out, start_out,
    flat, outgoing, from_depth, middle, gathered, m2_all, m2_t, core, pairs, gram, start_all,
    from_core, part, from_group, reduced, total,
    x_send, x_recv, z_send, z_recv, y_send, y_recv, m_send, m_recv, s_send, s_recv,
    c_send, c_recv, g_send, g_recv,
):
    n_row, n_col, n_depth = sizes
    width2, rows, width3 = cube_ref.shape
    per = middle.shape[2]
    count = n_depth * n_col * per
    rank2 = m2_ref.shape[1]
    half2 = rank2 // n_row
    row, col, depth = lax.axis_index("row"), lax.axis_index("col"), lax.axis_index("depth")
    n_z = n_col // 2
    z, parity = col // 2, col % 2
    other_row, other_depth = 1 - row, 1 - depth

    barrier = pltpu.get_barrier_semaphore()
    others = 0
    for dr in range(n_row):
        for dc in range(n_col):
            for dd in range(n_depth):
                if dr or dc or dd:
                    target = ((row + dr) % n_row, (col + dc) % n_col, (depth + dd) % n_depth)
                    pl.semaphore_signal(barrier, inc=1, device_id=target, device_id_type=MESH)
                    others += 1
    pl.semaphore_wait(barrier, others)

    started = []

    def send(src, dst, send_sem, recv_sem, target):
        copy = pltpu.make_async_remote_copy(
            src_ref=src, dst_ref=dst, send_sem=send_sem, recv_sem=recv_sem,
            device_id=target, device_id_type=MESH,
        )
        copy.start()
        started.append(copy)
        return copy

    own2 = pl.ds(pl.multiple_of(col * width2, width2), width2)
    m_copies = [
        send(m2_ref, m2_all.at[own2, :], m_send.at[o], m_recv.at[o], (row, (col + o) % n_col, depth))
        for o in range(1, n_col)
    ]
    own_rows = pl.ds(pl.multiple_of(row * rows, rows), rows)
    s_copy = send(start_ref, start_all.at[own_rows, :], s_send, s_recv, (other_row, col, depth))
    m2_all[own2, :] = m2_ref[...]
    start_all[own_rows, :] = start_ref[...]
    gram[...] = jnp.zeros_like(gram)
    x_copies, z_copies, y_copies = {}, {}, {}

    def first(q):
        def multiply(j, carry):
            tile = dot(m3_ref[q], cube_ref[j], 1, 1, None)
            for h in range(rows // 128):
                flat[h, pl.ds(j, count, stride=width2), :] = tile[:, h * 128 : h * 128 + 128]
            return carry

        lax.fori_loop(0, width2, multiply, 0, unroll=4)
        for d in range(n_depth):

            def store(t, carry):
                at = pl.ds(pl.multiple_of((d * n_col * per + t) * width2, width2), width2)
                for h in range(rows // 128):
                    outgoing[q, d, t, :, h * 128 : h * 128 + 128] = flat[h, at, :].astype(jnp.bfloat16)
                return carry

            lax.fori_loop(0, n_col * per, store, 0)
        x_copies[q] = send(
            outgoing.at[q, other_depth], from_depth.at[q], x_send.at[q], x_recv.at[q],
            (row, col, other_depth),
        )

    def second(q):
        x_copies[q].wait_recv()

        for c in range(n_col):
            for t in range(per):
                a = outgoing[q, depth, c * per + t].astype(jnp.float32)
                b = from_depth[q, c * per + t].astype(jnp.float32)
                middle[q, c, t] = (a + b).astype(jnp.bfloat16)
        z_copies[q] = []
        for o in range(1, n_col):
            to = (col + o) % n_col
            z_copies[q].append(
                send(
                    middle.at[q, to], gathered.at[q, :, own2, :], z_send.at[q, o], z_recv.at[q, o],
                    (row, to, depth),
                )
            )
        gathered[q, :, own2, :] = middle[q, col]

    def third(q):
        if q == 0:
            for copy in m_copies:
                copy.wait_recv()
            m2_t[...] = m2_all[...].astype(jnp.float32).T.astype(jnp.bfloat16)
        for copy in z_copies[q]:
            copy.wait_recv()

        def multiply(t, carry):
            core[q, t] = dot(m2_t[...], gathered[q, t], 1, 0, None).astype(jnp.bfloat16)
            return carry

        lax.fori_loop(0, per, multiply, 0)
        mine = pl.ds(pl.multiple_of(row * half2, half2), half2)
        theirs = pl.ds(pl.multiple_of(other_row * half2, half2), half2)
        lanes = pl.ds(pl.multiple_of(row * rows, rows), rows)
        y_copies[q] = send(
            core.at[q, :, theirs, :], pairs.at[q, :, :, lanes], y_send.at[q], y_recv.at[q],
            (other_row, col, depth),
        )
        pairs[q, :, :, lanes] = core[q, :, mine, :]

    def fourth(q):
        y_copies[q].wait_recv()
        x = pairs[q].reshape(per * half2, n_row * rows)
        low, high = x[:, :rows], x[:, rows:]
        gram[:rows, :] += dot(low, low, 0, 0, None)
        gram[rows : 2 * rows, :] += dot(high, low, 0, 0, None)
        gram[2 * rows :, :] += dot(high, high, 0, 0, None)

    stages = [first, second, third, fourth]
    for wave in range(CHUNKS + 3):
        for stage in range(4):
            if 0 <= wave - stage < CHUNKS:
                stages[stage](wave - stage)

    length = gram.shape[0]
    half = length // 2
    piece = half // (n_row * n_z * n_depth)

    def group(r, zz, d):
        return (r * n_z + zz) * n_depth + d

    keep = pl.ds(pl.multiple_of(parity * half, half), half)
    give = pl.ds(pl.multiple_of((1 - parity) * half, half), half)
    partner = (row, z * 2 + 1 - parity, depth)
    copy = send(gram.at[give, :], from_core, c_send.at[0], c_recv.at[0], partner)
    copy.wait_recv()
    part[...] = gram[keep, :] + from_core[...]
    offsets = [
        (dr, dz, dd)
        for dz in range(n_z) for dr in range(n_row) for dd in range(n_depth) if dr or dz or dd
    ]
    me = group(row, z, depth)
    copies = []
    for k, (dr, dz, dd) in enumerate(offsets):
        r, zz, d = (row + dr) % n_row, (z + dz) % n_z, (depth + dd) % n_depth
        at = pl.ds(pl.multiple_of(group(r, zz, d) * piece, piece), piece)
        copies.append(
            send(part.at[at, :], from_group.at[k], g_send.at[0, k], g_recv.at[0, k], (r, zz * 2 + parity, d))
        )
    value = part[pl.ds(pl.multiple_of(me * piece, piece), piece), :]
    for k, copy in enumerate(copies):
        copy.wait_recv()
        value = value + from_group[k]
    reduced[...] = value
    here = pl.ds(pl.multiple_of(parity * half + me * piece, piece), piece)
    copies = []
    for k, (dr, dz, dd) in enumerate(offsets):
        r, zz, d = (row + dr) % n_row, (z + dz) % n_z, (depth + dd) % n_depth
        copies.append(
            send(reduced, total.at[here, :], g_send.at[1, k], g_recv.at[1, k], (r, zz * 2 + parity, d))
        )
    total[here, :] = value
    for copy in copies:
        copy.wait_recv()
    copy = send(total.at[keep, :], total.at[keep, :], c_send.at[1], c_recv.at[1], partner)
    s_copy.wait_recv()
    start_out[...] = start_all[...]
    copy.wait_recv()
    cross = total[rows : 2 * rows, :]
    gram_out[:rows, :rows] = total[:rows, :]
    gram_out[rows:, :rows] = cross
    gram_out[:rows, rows:] = cross.T
    gram_out[rows:, rows:] = total[2 * rows :, :]
    for copy in started:
        copy.wait_send()


def exchange(sizes, cube, mode3_factor, mode2_factor, start_basis):
    n_row, n_col, n_depth = sizes
    rows, width2, width3 = cube.shape
    rank3, rank2 = mode3_factor.shape[1], mode2_factor.shape[1]
    per = rank3 // (n_depth * n_col * CHUNKS)
    cube_t = jnp.swapaxes(cube, 0, 1)
    m3 = mode3_factor.T.reshape(n_depth, n_col, CHUNKS, per, width3)
    m3 = m3.transpose(2, 0, 1, 3, 4).reshape(CHUNKS, n_depth * n_col * per, width3)
    length, half2 = n_row * rows, rank2 // n_row
    blocks = 3 * rows
    count = n_depth * n_col * per
    group = n_row * n_col // 2 * n_depth
    piece = blocks // 2 // group
    bf16, f32, dma = jnp.bfloat16, jnp.float32, pltpu.SemaphoreType.DMA
    vmem = pl.BlockSpec(memory_space=pltpu.VMEM)
    return pl.pallas_call(
        functools.partial(exchange_kernel, sizes),
        out_shape=[
            jax.ShapeDtypeStruct((length, length), f32),
            jax.ShapeDtypeStruct((length, start_basis.shape[1]), f32),
        ],
        in_specs=[vmem] * 4,
        out_specs=[vmem] * 2,
        scratch_shapes=[
            pltpu.VMEM((rows // 128, count * width2, 128), f32),
            pltpu.VMEM((CHUNKS, n_depth, n_col * per, width2, rows), bf16),
            pltpu.VMEM((CHUNKS, n_col * per, width2, rows), bf16),
            pltpu.VMEM((CHUNKS, n_col, per, width2, rows), bf16),
            pltpu.VMEM((CHUNKS, per, n_col * width2, rows), bf16),
            pltpu.VMEM((n_col * width2, rank2), bf16),
            pltpu.VMEM((rank2, n_col * width2), bf16),
            pltpu.VMEM((CHUNKS, per, rank2, rows), bf16),
            pltpu.VMEM((CHUNKS, per, half2, length), bf16),
            pltpu.VMEM((blocks, rows), f32),
            pltpu.VMEM((length, start_basis.shape[1]), f32),
            pltpu.VMEM((blocks // 2, rows), f32),
            pltpu.VMEM((blocks // 2, rows), f32),
            pltpu.VMEM((group - 1, piece, rows), f32),
            pltpu.VMEM((piece, rows), f32),
            pltpu.VMEM((blocks, rows), f32),
            dma((CHUNKS,)), dma((CHUNKS,)), dma((CHUNKS, n_col)), dma((CHUNKS, n_col)),
            dma((CHUNKS,)), dma((CHUNKS,)), dma((n_col,)), dma((n_col,)), dma, dma,
            dma((2,)), dma((2,)), dma((2, group)), dma((2, group)),
        ],
        compiler_params=pltpu.CompilerParams(
            collective_id=0, has_side_effects=True, vmem_limit_bytes=60 * 2**20
        ),
        name="exchange",
    )(cube_t, m3, mode2_factor, start_basis)


def collectives(cube, mode3_factor, mode2_factor, start_basis):
    rows, width2, width3 = cube.shape
    rank = mode3_factor.shape[1]
    n_depth = lax.axis_size("depth")
    flat = cube.reshape(rows * width2, width3)
    rank3 = rank // n_depth
    middle = lax.psum_scatter(
        lax.dot_general(
            mode3_factor, flat, (((0,), (1,)), ((), ())), preferred_element_type=jnp.float32
        ).astype(jnp.bfloat16),
        "depth",
        scatter_dimension=0,
        tiled=True,
    )
    middle = middle.reshape(rank3, rows, width2)
    middle = lax.all_to_all(middle, "col", 0, 2, tiled=True)
    factor2 = lax.all_gather(mode2_factor, "col", axis=0, tiled=True)
    core = jnp.einsum("tij,jr->tri", middle, factor2, preferred_element_type=jnp.float32)
    core = core.astype(jnp.bfloat16)
    core = lax.all_to_all(core, "row", 1, 2, tiled=True)
    core = core.reshape(-1, core.shape[2])
    gram = lax.psum(dot(core, core, 0, 0, None), ("row", "col", "depth"))
    start = lax.all_gather(start_basis, "row", axis=0, tiled=True)
    return gram, start


def shards(cube, mode3_factor, mode2_factor, start_basis):
    rows = cube.shape[0]
    sizes = tuple(lax.axis_size(name) for name in ("row", "col", "depth"))
    if sizes[0] == 2 and sizes[2] == 2 and rows % 128 == 0 and rows * 3 % (16 * sizes[1] * 2) == 0:
        gram, start = exchange(sizes, cube, mode3_factor, mode2_factor, start_basis)
    else:
        gram, start = collectives(cube, mode3_factor, mode2_factor, start_basis)
    basis = subspace(gram, start)
    return lax.dynamic_slice_in_dim(basis, lax.axis_index("row") * rows, rows, 0)


def solution(mesh):
    in_specs = (P("row", "col", "depth"), P("depth", None), P("col", None), P("row", None))
    out_specs = P("row", None)
    return jax.shard_map(shards, mesh=mesh, in_specs=in_specs, out_specs=out_specs, check_vma=False)
```

```python
import functools
import math

import jax
import jax.numpy as jnp
from jax import lax
from jax.experimental import pallas as pl
from jax.experimental.pallas import tpu as pltpu
from jax.sharding import PartitionSpec as P

ITERS = 4
OUTER = 128
HIGHEST = lax.Precision.HIGHEST


def dot(a, b, ca, cb, precision=HIGHEST):
    return lax.dot_general(
        a, b, (((ca,), (cb,)), ((), ())), precision=precision, preferred_element_type=jnp.float32
    )


def block_inverse(block):
    n = OUTER
    lane = lax.broadcasted_iota(jnp.int32, (n, n), 1)
    sub = lax.broadcasted_iota(jnp.int32, (n, n), 0)
    eye = jnp.where(lane == sub, 1.0, 0.0).astype(jnp.float32)
    whole = jnp.concatenate([block, eye], axis=1)
    tiles = [whole[8 * v : 8 * v + 8, :] for v in range(n // 8)]
    sublane = lax.broadcasted_iota(jnp.int32, (8, 2 * n), 0)
    full = (8, 2 * n)
    for b in range(n // 8):
        tile = tiles[b]
        d = {}
        for j in range(8):
            column = jnp.broadcast_to(tile[:, 8 * b + j : 8 * b + j + 1], full)
            for i in range(j, 8):
                d[i, j] = jnp.broadcast_to(column[i : i + 1, :], full)
        rows = [jnp.broadcast_to(tile[k : k + 1, :], full) for k in range(8)]
        low, p, reduced = {}, [], []
        for j in range(8):
            p.append(lax.rsqrt(d[j, j]))
            for i in range(j + 1, 8):
                low[i, j] = d[i, j] * p[j]
            for k in range(j + 1, 8):
                for i in range(k, 8):
                    d[i, k] = d[i, k] - low[i, j] * low[k, j]
            row = rows[j] * p[j]
            reduced.append(row)
            for i in range(j + 1, 8):
                rows[i] = rows[i] - low[i, j] * row
        out = reduced[0]
        for k in range(1, 8):
            out = jnp.where(sublane == k, reduced[k], out)
        tiles[b] = out
        if b < n // 8 - 1:
            solved = list(reduced)
            for k in range(7, -1, -1):
                solved[k] = solved[k] * p[k]
                for m in range(k):
                    solved[m] = solved[m] - low[k, m] * solved[k]
            for v in range(b + 1, n // 8):
                old = tiles[v]
                new = old
                for k in range(8):
                    new = new - jnp.broadcast_to(old[:, 8 * b + k : 8 * b + k + 1], full) * solved[k]
                tiles[v] = new
    return jnp.concatenate(tiles, axis=0)[:, n:]


def subspace_kernel(gram_ref, start_ref, out_ref, image_ref, work_ref, block_ref):
    size = start_ref.shape[1]
    out_ref[...] = start_ref[...]
    blocks = size // OUTER

    def iteration(step, carry):
        image_ref[...] = dot(gram_ref[...], out_ref[...], 1, 0)
        image = image_ref[...]
        work_ref[:, :size] = dot(image, image, 0, 0)
        lane = lax.broadcasted_iota(jnp.int32, (size, size), 1)
        sub = lax.broadcasted_iota(jnp.int32, (size, size), 0)
        work_ref[:, size:] = jnp.where(lane == sub, 1.0, 0.0).astype(jnp.float32)
        block_ref[...] = work_ref[:OUTER, :OUTER]

        def outer(o, carry):
            inverse = block_inverse(block_ref[...])
            for s in range(blocks):

                @pl.when(o == s)
                def _():
                    low, high = s * OUTER, (s + 1) * OUTER
                    rows = dot(inverse, work_ref[low:high, high : size + high], 1, 0)
                    work_ref[low:high, high : size + high] = rows
                    if s < blocks - 1:
                        update = dot(rows[:, : size - high], rows, 0, 0)
                        work_ref[high:, high : size + high] -= update
                        block_ref[...] = work_ref[high : high + OUTER, high : high + OUTER]

            return carry

        lax.fori_loop(0, blocks, outer, 0)
        scale = jnp.where(step == ITERS - 1, math.sqrt(gram_ref.shape[0]), 1.0).astype(jnp.float32)
        out_ref[...] = dot(image_ref[...], work_ref[:, size:], 1, 1) * scale
        return carry

    lax.fori_loop(0, ITERS, iteration, 0)


def subspace(gram, start):
    length, size = start.shape
    return pl.pallas_call(
        subspace_kernel,
        out_shape=jax.ShapeDtypeStruct((length, size), jnp.float32),
        in_specs=[pl.BlockSpec(memory_space=pltpu.VMEM)] * 2,
        out_specs=pl.BlockSpec(memory_space=pltpu.VMEM),
        scratch_shapes=[
            pltpu.VMEM((length, size), jnp.float32),
            pltpu.VMEM((size, 2 * size), jnp.float32),
            pltpu.VMEM((OUTER, OUTER), jnp.float32),
        ],
        compiler_params=pltpu.CompilerParams(vmem_limit_bytes=40 * 2**20),
        name="subspace",
    )(gram, start)


CHUNKS = 8
MESH = pl.DeviceIdType.MESH


def exchange_kernel(
    sizes, cube_ref, m3_ref, m2_ref, start_ref, gram_out, start_out,
    flat, outgoing, from_depth, middle, gathered, m2_all, m2_t, core, pairs, gram, start_all,
    from_core, part, from_group, reduced, total,
    x_send, x_recv, z_send, z_recv, y_send, y_recv, m_send, m_recv, s_send, s_recv,
    c_send, c_recv, g_send, g_recv,
):
    n_row, n_col, n_depth = sizes
    width2, rows, width3 = cube_ref.shape
    per = middle.shape[2]
    count = n_depth * n_col * per
    rank2 = m2_ref.shape[1]
    half2 = rank2 // n_row
    row, col, depth = lax.axis_index("row"), lax.axis_index("col"), lax.axis_index("depth")
    n_z = n_col // 2
    z, parity = col // 2, col % 2
    other_row, other_depth = 1 - row, 1 - depth

    barrier = pltpu.get_barrier_semaphore()
    others = 0
    for dr in range(n_row):
        for dc in range(n_col):
            for dd in range(n_depth):
                if dr or dc or dd:
                    target = ((row + dr) % n_row, (col + dc) % n_col, (depth + dd) % n_depth)
                    pl.semaphore_signal(barrier, inc=1, device_id=target, device_id_type=MESH)
                    others += 1
    pl.semaphore_wait(barrier, others)

    started = []

    def send(src, dst, send_sem, recv_sem, target):
        copy = pltpu.make_async_remote_copy(
            src_ref=src, dst_ref=dst, send_sem=send_sem, recv_sem=recv_sem,
            device_id=target, device_id_type=MESH,
        )
        copy.start()
        started.append(copy)
        return copy

    own2 = pl.ds(pl.multiple_of(col * width2, width2), width2)
    m_copies = [
        send(m2_ref, m2_all.at[own2, :], m_send.at[o], m_recv.at[o], (row, (col + o) % n_col, depth))
        for o in range(1, n_col)
    ]
    own_rows = pl.ds(pl.multiple_of(row * rows, rows), rows)
    s_copy = send(start_ref, start_all.at[own_rows, :], s_send, s_recv, (other_row, col, depth))
    m2_all[own2, :] = m2_ref[...]
    start_all[own_rows, :] = start_ref[...]
    gram[...] = jnp.zeros_like(gram)
    x_copies, z_copies, y_copies = {}, {}, {}

    def first(q):
        def multiply(j, carry):
            tile = dot(m3_ref[q], cube_ref[j], 1, 1, None)
            for h in range(rows // 128):
                flat[h, pl.ds(j, count, stride=width2), :] = tile[:, h * 128 : h * 128 + 128]
            return carry

        lax.fori_loop(0, width2, multiply, 0, unroll=4)
        for d in range(n_depth):

            def store(t, carry):
                at = pl.ds(pl.multiple_of((d * n_col * per + t) * width2, width2), width2)
                for h in range(rows // 128):
                    outgoing[q, d, t, :, h * 128 : h * 128 + 128] = flat[h, at, :].astype(jnp.bfloat16)
                return carry

            lax.fori_loop(0, n_col * per, store, 0)
        x_copies[q] = send(
            outgoing.at[q, other_depth], from_depth.at[q], x_send.at[q], x_recv.at[q],
            (row, col, other_depth),
        )

    def second(q):
        x_copies[q].wait_recv()

        for c in range(n_col):
            for t in range(per):
                a = outgoing[q, depth, c * per + t].astype(jnp.float32)
                b = from_depth[q, c * per + t].astype(jnp.float32)
                middle[q, c, t] = (a + b).astype(jnp.bfloat16)
        z_copies[q] = []
        for o in range(1, n_col):
            to = (col + o) % n_col
            z_copies[q].append(
                send(
                    middle.at[q, to], gathered.at[q, :, own2, :], z_send.at[q, o], z_recv.at[q, o],
                    (row, to, depth),
                )
            )
        gathered[q, :, own2, :] = middle[q, col]

    def third(q):
        if q == 0:
            for copy in m_copies:
                copy.wait_recv()
            m2_t[...] = m2_all[...].astype(jnp.float32).T.astype(jnp.bfloat16)
        for copy in z_copies[q]:
            copy.wait_recv()

        def multiply(t, carry):
            core[q, t] = dot(m2_t[...], gathered[q, t], 1, 0, None).astype(jnp.bfloat16)
            return carry

        lax.fori_loop(0, per, multiply, 0)
        mine = pl.ds(pl.multiple_of(row * half2, half2), half2)
        theirs = pl.ds(pl.multiple_of(other_row * half2, half2), half2)
        lanes = pl.ds(pl.multiple_of(row * rows, rows), rows)
        y_copies[q] = send(
            core.at[q, :, theirs, :], pairs.at[q, :, :, lanes], y_send.at[q], y_recv.at[q],
            (other_row, col, depth),
        )
        pairs[q, :, :, lanes] = core[q, :, mine, :]

    def fourth(q):
        y_copies[q].wait_recv()
        x = pairs[q].reshape(per * half2, n_row * rows)
        low, high = x[:, :rows], x[:, rows:]
        gram[:rows, :] += dot(low, low, 0, 0, None)
        gram[rows : 2 * rows, :] += dot(high, low, 0, 0, None)
        gram[2 * rows :, :] += dot(high, high, 0, 0, None)

    stages = [first, second, third, fourth]
    for wave in range(CHUNKS + 3):
        for stage in range(4):
            if 0 <= wave - stage < CHUNKS:
                stages[stage](wave - stage)

    length = gram.shape[0]
    half = length // 2
    piece = half // (n_row * n_z * n_depth)

    def group(r, zz, d):
        return (r * n_z + zz) * n_depth + d

    keep = pl.ds(pl.multiple_of(parity * half, half), half)
    give = pl.ds(pl.multiple_of((1 - parity) * half, half), half)
    partner = (row, z * 2 + 1 - parity, depth)
    copy = send(gram.at[give, :], from_core, c_send.at[0], c_recv.at[0], partner)
    copy.wait_recv()
    part[...] = gram[keep, :] + from_core[...]
    offsets = [
        (dr, dz, dd)
        for dz in range(n_z) for dr in range(n_row) for dd in range(n_depth) if dr or dz or dd
    ]
    me = group(row, z, depth)
    copies = []
    for k, (dr, dz, dd) in enumerate(offsets):
        r, zz, d = (row + dr) % n_row, (z + dz) % n_z, (depth + dd) % n_depth
        at = pl.ds(pl.multiple_of(group(r, zz, d) * piece, piece), piece)
        copies.append(
            send(part.at[at, :], from_group.at[k], g_send.at[0, k], g_recv.at[0, k], (r, zz * 2 + parity, d))
        )
    value = part[pl.ds(pl.multiple_of(me * piece, piece), piece), :]
    for k, copy in enumerate(copies):
        copy.wait_recv()
        value = value + from_group[k]
    reduced[...] = value
    here = pl.ds(pl.multiple_of(parity * half + me * piece, piece), piece)
    copies = []
    for k, (dr, dz, dd) in enumerate(offsets):
        r, zz, d = (row + dr) % n_row, (z + dz) % n_z, (depth + dd) % n_depth
        copies.append(
            send(reduced, total.at[here, :], g_send.at[1, k], g_recv.at[1, k], (r, zz * 2 + parity, d))
        )
    total[here, :] = value
    for copy in copies:
        copy.wait_recv()
    copy = send(total.at[keep, :], total.at[keep, :], c_send.at[1], c_recv.at[1], partner)
    s_copy.wait_recv()
    start_out[...] = start_all[...]
    copy.wait_recv()
    cross = total[rows : 2 * rows, :]
    gram_out[:rows, :rows] = total[:rows, :]
    gram_out[rows:, :rows] = cross
    gram_out[:rows, rows:] = cross.T
    gram_out[rows:, rows:] = total[2 * rows :, :]
    for copy in started:
        copy.wait_send()


def exchange(sizes, cube, mode3_factor, mode2_factor, start_basis):
    n_row, n_col, n_depth = sizes
    rows, width2, width3 = cube.shape
    rank3, rank2 = mode3_factor.shape[1], mode2_factor.shape[1]
    per = rank3 // (n_depth * n_col * CHUNKS)
    cube_t = jnp.swapaxes(cube, 0, 1)
    m3 = mode3_factor.T.reshape(n_depth, n_col, CHUNKS, per, width3)
    m3 = m3.transpose(2, 0, 1, 3, 4).reshape(CHUNKS, n_depth * n_col * per, width3)
    length, half2 = n_row * rows, rank2 // n_row
    blocks = 3 * rows
    count = n_depth * n_col * per
    group = n_row * n_col // 2 * n_depth
    piece = blocks // 2 // group
    bf16, f32, dma = jnp.bfloat16, jnp.float32, pltpu.SemaphoreType.DMA
    vmem = pl.BlockSpec(memory_space=pltpu.VMEM)
    return pl.pallas_call(
        functools.partial(exchange_kernel, sizes),
        out_shape=[
            jax.ShapeDtypeStruct((length, length), f32),
            jax.ShapeDtypeStruct((length, start_basis.shape[1]), f32),
        ],
        in_specs=[vmem] * 4,
        out_specs=[vmem] * 2,
        scratch_shapes=[
            pltpu.VMEM((rows // 128, count * width2, 128), f32),
            pltpu.VMEM((CHUNKS, n_depth, n_col * per, width2, rows), bf16),
            pltpu.VMEM((CHUNKS, n_col * per, width2, rows), bf16),
            pltpu.VMEM((CHUNKS, n_col, per, width2, rows), bf16),
            pltpu.VMEM((CHUNKS, per, n_col * width2, rows), bf16),
            pltpu.VMEM((n_col * width2, rank2), bf16),
            pltpu.VMEM((rank2, n_col * width2), bf16),
            pltpu.VMEM((CHUNKS, per, rank2, rows), bf16),
            pltpu.VMEM((CHUNKS, per, half2, length), bf16),
            pltpu.VMEM((blocks, rows), f32),
            pltpu.VMEM((length, start_basis.shape[1]), f32),
            pltpu.VMEM((blocks // 2, rows), f32),
            pltpu.VMEM((blocks // 2, rows), f32),
            pltpu.VMEM((group - 1, piece, rows), f32),
            pltpu.VMEM((piece, rows), f32),
            pltpu.VMEM((blocks, rows), f32),
            dma((CHUNKS,)), dma((CHUNKS,)), dma((CHUNKS, n_col)), dma((CHUNKS, n_col)),
            dma((CHUNKS,)), dma((CHUNKS,)), dma((n_col,)), dma((n_col,)), dma, dma,
            dma((2,)), dma((2,)), dma((2, group)), dma((2, group)),
        ],
        compiler_params=pltpu.CompilerParams(
            collective_id=0, has_side_effects=True, vmem_limit_bytes=60 * 2**20
        ),
        name="exchange",
    )(cube_t, m3, mode2_factor, start_basis)


def collectives(cube, mode3_factor, mode2_factor, start_basis):
    rows, width2, width3 = cube.shape
    rank = mode3_factor.shape[1]
    n_depth = lax.axis_size("depth")
    flat = cube.reshape(rows * width2, width3)
    rank3 = rank // n_depth
    middle = lax.psum_scatter(
        lax.dot_general(
            mode3_factor, flat, (((0,), (1,)), ((), ())), preferred_element_type=jnp.float32
        ).astype(jnp.bfloat16),
        "depth",
        scatter_dimension=0,
        tiled=True,
    )
    middle = middle.reshape(rank3, rows, width2)
    middle = lax.all_to_all(middle, "col", 0, 2, tiled=True)
    factor2 = lax.all_gather(mode2_factor, "col", axis=0, tiled=True)
    core = jnp.einsum("tij,jr->tri", middle, factor2, preferred_element_type=jnp.float32)
    core = core.astype(jnp.bfloat16)
    core = lax.all_to_all(core, "row", 1, 2, tiled=True)
    core = core.reshape(-1, core.shape[2])
    gram = lax.psum(dot(core, core, 0, 0, None), ("row", "col", "depth"))
    start = lax.all_gather(start_basis, "row", axis=0, tiled=True)
    return gram, start


def shards(cube, mode3_factor, mode2_factor, start_basis):
    rows = cube.shape[0]
    sizes = tuple(lax.axis_size(name) for name in ("row", "col", "depth"))
    if sizes[0] == 2 and sizes[2] == 2 and rows % 128 == 0 and rows * 3 % (16 * sizes[1] * 2) == 0:
        gram, start = exchange(sizes, cube, mode3_factor, mode2_factor, start_basis)
    else:
        gram, start = collectives(cube, mode3_factor, mode2_factor, start_basis)
    basis = subspace(gram, start)
    return lax.dynamic_slice_in_dim(basis, lax.axis_index("row") * rows, rows, 0)


def solution(mesh):
    in_specs = (P("row", "col", "depth"), P("depth", None), P("col", None), P("row", None))
    out_specs = P("row", None)
    return jax.shard_map(shards, mesh=mesh, in_specs=in_specs, out_specs=out_specs, check_vma=False)
```
